32 devices in a mesh: seq: 8 (over z, x), grp: 4 (over y, core).
Axes of the slice: x: 2, y: 2, z: 4, core: 2. Of those that a mesh axis runs over, the one named last changes fastest.
Arguments:
- x_input: bfloat16 [4, 1024, 2880], P('grp', 'seq'), may hold values from -6 to 6
- q_input: bfloat16 [4, 1024, 2048], P('grp', 'seq'), may hold values from -6.5 to 6.5
- k_input: bfloat16 [4, 1024, 256], P('grp', 'seq'), may hold values from -6.5 to 6.5
- v_input: bfloat16 [4, 1024, 256], P('grp', 'seq'), may hold values from -6 to 6
- out_weight: bfloat16 [2048, 2880], P('seq'), may hold values from -0.125 to 0.125
- norm_gain: float32 [2880], replicated, may hold values from 0.1 to 1.9
- expert_ids: int32 [4, 1024, 4], P('grp', 'seq'), may hold values from 0 to 31, all different within a row; in each aligned block of 128 rows (0 to 127, 128 to 255, ..., all dimensions but the last counted through in order) at most 32 rows name the same one
- route_weights: float32 [4, 1024, 4], P('grp', 'seq'), may hold values from 0.2 to 1
- gate_weights: bfloat16 [32, 2880, 1440], P(('seq', 'grp')), may hold values from -0.109375 to 0.109375
- up_weights: bfloat16 [32, 2880, 1440], P(('seq', 'grp')), may hold values from -0.109375 to 0.109375
- down_weights: bfloat16 [32, 1440, 2880], P(('seq', 'grp')), may hold values from -0.15625 to 0.15625
Outputs:
- layer_out: bfloat16 [4, 1024, 2880], P('grp', 'seq')
The draws below stay inside these ranges and needn't reach their ends.
Inputs may be any that keep to these rules, and one draw needn't show every extreme that they name: `expert_ids`: each row names 4 different experts; within the rows of one device no expert is named by more than 32 rows.
All inputs are finite; a program needn't handle non-finite values.
Results may differ from the reference program's by a relative error of at most 0.013.
Values may be sent and summed in bfloat16 or wider, within the bound.
A program may use at most 128 MiB of HBM per device.

```python
import math
import jax
import jax.numpy as jnp
import numpy as np
from jax import lax

D = 2880
QH = 32
KVH = 4
HEAD = 64
WINDOW = 128
HID = 1440
TOP = 4
TOK_DEV = 128
SEQS = 4
SEQ_LEN = 1024
EXPERTS = 32
MOST = 32
N_SEQ = 8
N_GRP = 4


def draw_k_input(key, part):
    values = jax.random.truncated_normal(jax.random.fold_in(key, 11), -4.0, 4.0, (SEQS, SEQ_LEN, KVH, HEAD), jnp.float32)
    return values.reshape(SEQS, SEQ_LEN, KVH * HEAD).astype(jnp.bfloat16)


def draw_q_input(key, part):
    group = QH // KVH
    values = jax.random.truncated_normal(jax.random.fold_in(key, 13), -4.0, 4.0, (SEQS, SEQ_LEN, KVH, group, HEAD), jnp.float32)
    return values.reshape(SEQS, SEQ_LEN, QH * HEAD).astype(jnp.bfloat16)


def block_levels(rng, shape, cuts, low, largest):
    def one(axis_at, blocks):
        heights = jax.random.uniform(jax.random.fold_in(jax.random.fold_in(rng, 6), axis_at), (blocks,), jnp.float32, low / len(cuts), largest / len(cuts))
        return jnp.repeat(jnp.exp(heights), shape[axis_at] // blocks).reshape((-1,) + (1,) * (len(shape) - axis_at - 1))

    gain = one(*cuts[0])
    for cut in cuts[1:]:
        gain = gain * one(*cut)
    return gain


def routed_block(stream_key, own, number, rows, amount, top, bound, skew):
    sequence = jax.random.permutation(stream_key, amount)
    packed, ordinary = load_shares(amount, rows * top, bound, skew, True), load_shares(amount, rows * top, bound, skew, False)
    places = jnp.arange(amount)

    def named(sizes, turn):
        used = int((sizes > 0).sum())
        fixed = max(1, used // 4)
        moved = fixed + (places - fixed + turn * (used - fixed)) % max(1, amount - fixed)
        return jnp.zeros((amount,), jnp.int32).at[sequence[jnp.where(places < fixed, places, moved)]].set(jnp.asarray(sizes, jnp.int32))

    sizes = jnp.where(number % 4 == 0, named(packed, number // 4), named(ordinary, number - number // 4 - 1))
    mixed = jax.random.permutation(jax.random.fold_in(own, 3), amount)
    giver, taker = mixed[0:amount // 2 * 2:2], mixed[1:amount // 2 * 2:2]
    slack = jnp.minimum(sizes[giver] - 1, bound - sizes[taker]) // 2
    slack = jnp.where((giver == sequence[0]) | (taker == sequence[0]) | (sizes[taker] == 0), 0, jnp.maximum(slack, 0))
    moved = jax.random.randint(jax.random.fold_in(own, 4), (amount // 2,), 0, 1 << 20) % (slack + 1)
    sizes = sizes.at[giver].add(-moved).at[taker].add(moved)
    items = jnp.searchsorted(jnp.cumsum(sizes), jnp.arange(rows * top), side="right").astype(jnp.int32)
    listing = items.reshape(top, rows).T
    listing = listing[jax.random.permutation(jax.random.fold_in(own, 1), rows)]
    turn = jax.random.randint(jax.random.fold_in(own, 2), (rows, 1), 0, top)
    return jnp.take_along_axis(listing, (jnp.arange(top)[None, :] + turn) % top, axis=1)


def load_shares(amount, total, reach, skew, full):
    weights = [(1 << 20) // math.isqrt(grade ** skew) + 1 for grade in range(1, amount + 1)]
    largest = reach if full else min(reach, max(-(-total // amount), total * weights[0] // sum(weights)))
    least = 1 if total - largest >= amount - 1 else 0
    holding, surplus = [largest] + [least] * (amount - 1), total - largest - least * (amount - 1)
    while surplus > 0:
        candidates = [i for i in range(1, amount) if holding[i] < largest] or [i for i in range(1, amount) if holding[i] < reach]
        mass, remaining = sum([weights[i] for i in candidates]), surplus
        for i in candidates:
            extra = min(reach - holding[i], max(1, remaining * weights[i] // mass), surplus)
            holding[i] = holding[i] + extra
            surplus = surplus - extra
    return np.array(holding)


def gaussian(stream_key, shape, deviation, reach, cuts=(), kind=jnp.bfloat16):
    values = jax.random.normal(stream_key, shape, jnp.float32) * deviation
    if len(cuts) > 0:
        values = block_levels(stream_key, shape, cuts, -0.22, 0.18) * values
    return jnp.clip(values, min=-reach, max=reach).astype(kind)


def setup_inputs(seed: int = 0) -> dict:
    arg_keys = jax.random.split(jax.random.key(seed), 12)
    x_input = gaussian(arg_keys[0], (SEQS, SEQ_LEN, D), 1.0, 6.0, ((0, 4), (1, 8)))
    q_input = draw_q_input(jax.random.fold_in(arg_keys[11], 71), 0)
    k_input = draw_k_input(jax.random.fold_in(arg_keys[11], 71), 0)
    v_input = gaussian(arg_keys[3], (SEQS, SEQ_LEN, KVH * HEAD), 1.0, 6.0, ((0, 4), (1, 8)))
    out_weight = gaussian(arg_keys[4], (QH * HEAD, D), (QH * HEAD) ** -0.5, 0.125, ((0, 8),))
    norm_gain = jnp.clip(1.0 + 0.18 * jax.random.normal(arg_keys[5], (D,), jnp.float32), 0.1, 1.9)
    expert_ids_keys = jax.random.split(jax.random.fold_in(arg_keys[6], 1), SEQS * SEQ_LEN // TOK_DEV)
    expert_ids_turns = jax.random.permutation(jax.random.fold_in(arg_keys[6], 3), SEQS * SEQ_LEN // TOK_DEV)
    expert_ids = jax.vmap(lambda own, number: routed_block(jax.random.fold_in(arg_keys[6], 2), own, number, TOK_DEV, EXPERTS, TOP, MOST, 2))(expert_ids_keys, expert_ids_turns).reshape((SEQS, SEQ_LEN, TOP))
    route_weights = jnp.clip(0.2 + 0.8 * jax.random.uniform(arg_keys[7], (SEQS, SEQ_LEN, TOP), jnp.float32) ** block_levels(arg_keys[7], (SEQS, SEQ_LEN, TOP), ((0, 4), (1, 8)), -0.2, 0.2), 0.2, 1.0)
    gate_weights = gaussian(arg_keys[8], (EXPERTS, D, HID), D ** -0.5, 0.109375, ((0, 32),))
    up_weights = gaussian(arg_keys[9], (EXPERTS, D, HID), D ** -0.5, 0.109375, ((0, 32),))
    down_weights = gaussian(arg_keys[10], (EXPERTS, HID, D), HID ** -0.5, 0.15625, ((0, 32),))
    return dict(x_input=x_input, q_input=q_input, k_input=k_input, v_input=v_input, out_weight=out_weight, norm_gain=norm_gain, expert_ids=expert_ids, route_weights=route_weights, gate_weights=gate_weights, up_weights=up_weights, down_weights=down_weights)


def softmax_mix(scores, query_pos, key_pos, value_block):
    allowed = (key_pos[None, :] <= query_pos[:, None]) & (key_pos[None, :] > query_pos[:, None] - WINDOW) & (key_pos[None, :] >= 0)
    masked = jnp.where(allowed, scores, -jnp.inf)
    highest = lax.optimization_barrier(jnp.max(masked, axis=-1, keepdims=True))
    powers = jnp.exp(masked - highest)
    weights = (powers / lax.optimization_barrier(jnp.sum(powers, axis=-1, keepdims=True))).astype(jnp.bfloat16)
    mixed = jnp.einsum('kgts,skd->tkgd', weights.astype(jnp.float32), value_block)
    return mixed.astype(jnp.bfloat16)

def attend_sequence(operands):
    queries, keys, values = operands
    block = math.gcd(SEQ_LEN, 512)
    group = QH // KVH
    scale = 1.0 / math.sqrt(HEAD)
    padding = jnp.zeros((WINDOW, KVH * HEAD), jnp.bfloat16)
    key_rows = jnp.concatenate([padding, keys], 0)
    value_rows = jnp.concatenate([padding, values], 0)

    def one_block(block_index):
        first = block_index * block
        query_block = lax.dynamic_slice_in_dim(queries, first, block, 0).astype(jnp.float32).reshape(block, KVH, group, HEAD)
        key_block = lax.dynamic_slice_in_dim(key_rows, first, block + WINDOW, 0).astype(jnp.float32).reshape(block + WINDOW, KVH, HEAD)
        value_block = lax.dynamic_slice_in_dim(value_rows, first, block + WINDOW, 0).astype(jnp.float32).reshape(block + WINDOW, KVH, HEAD)
        scores = jnp.einsum('tkgd,skd->kgts', query_block, key_block) * scale
        query_pos = first + jnp.arange(block, dtype=jnp.int32)
        key_pos = first - WINDOW + jnp.arange(block + WINDOW, dtype=jnp.int32)
        return softmax_mix(scores, query_pos, key_pos, value_block).reshape(block, QH * HEAD)
    outputs = lax.map(one_block, jnp.arange(SEQ_LEN // block, dtype=jnp.int32))
    return outputs.reshape(SEQ_LEN, QH * HEAD)

def expert_mlp(rows, gate_matrix, up_matrix, down_matrix):
    gate = jnp.dot(rows, gate_matrix, preferred_element_type=jnp.float32)
    upward = jnp.dot(rows, up_matrix, preferred_element_type=jnp.float32)
    hidden = (gate * jax.nn.sigmoid(1.702 * gate) * (upward + 1.0)).astype(jnp.bfloat16)
    return jnp.dot(hidden, down_matrix, preferred_element_type=jnp.float32).astype(jnp.bfloat16)

def reference(x_input, q_input, k_input, v_input, out_weight, norm_gain, expert_ids, route_weights, gate_weights, up_weights, down_weights):
    attention = lax.map(attend_sequence, (q_input, k_input, v_input))
    flat_attention = attention.reshape(SEQS * SEQ_LEN, QH * HEAD)
    projected = jnp.dot(flat_attention, out_weight, preferred_element_type=jnp.float32)
    stream = x_input.reshape(SEQS * SEQ_LEN, D).astype(jnp.float32) + projected
    mean_square = lax.optimization_barrier(jnp.mean(stream * stream, axis=-1, keepdims=True))
    normed = (stream * lax.rsqrt(mean_square + 1e-05) * norm_gain).astype(jnp.bfloat16)
    flat_ids = expert_ids.reshape(-1)
    flat_weights = route_weights.reshape(-1)
    capacity = MOST * N_SEQ * N_GRP

    def per_expert(expert, totals):
        chosen = flat_ids == expert
        positions = jnp.nonzero(chosen, size=capacity, fill_value=0)[0].astype(jnp.int32)
        in_use = jnp.arange(capacity, dtype=jnp.int32) < jnp.sum(chosen.astype(jnp.int32))
        token_rows = positions // TOP
        served = expert_mlp(normed[token_rows], gate_weights[expert], up_weights[expert], down_weights[expert])
        scaled = served.astype(jnp.float32) * flat_weights[positions][:, None]
        contribution = jnp.where(in_use[:, None], scaled, jnp.zeros_like(scaled))
        return totals.at[token_rows].add(contribution)
    mixture = lax.fori_loop(0, EXPERTS, per_expert, jnp.zeros((SEQS * SEQ_LEN, D), jnp.float32))
    return (stream + mixture).astype(jnp.bfloat16).reshape(SEQS, SEQ_LEN, D)
```

```python
import functools
import math

import jax
import jax.numpy as jnp
from jax import lax
from jax.experimental import pallas as pl
from jax.experimental.pallas import tpu as pltpu
from jax.sharding import PartitionSpec as P

HEAD = 64
WINDOW = 128


def shifted(block, axis, distance):
    devices = range(lax.axis_size(axis))
    route = [(i - distance, i) for i in devices if i - distance in devices]
    return lax.ppermute(block, axis, route)


def softmax_mix(scores, query_pos, key_pos, value_block):
    allowed = (
        (key_pos[None, :] <= query_pos[:, None])
        & (key_pos[None, :] > query_pos[:, None] - WINDOW)
        & (key_pos[None, :] >= 0)
    )
    masked = jnp.where(allowed, scores, -jnp.inf)
    highest = jnp.max(masked, axis=-1, keepdims=True)
    powers = jnp.exp(masked - highest)
    weights = (powers / jnp.sum(powers, axis=-1, keepdims=True)).astype(jnp.bfloat16)
    return jnp.einsum(
        "kgts,skd->tkgd", weights, value_block, preferred_element_type=jnp.float32
    ).astype(jnp.bfloat16)


def expert_body(row_step, rows_ref, gate_ref, up_ref, down_ref, out_ref, total_ref):
    step = pl.program_id(0)
    last = pl.num_programs(0) - 1
    over_width = (((1,), (1,)), ((), ()))

    def row_block(index, carry):
        at = pl.ds(pl.multiple_of(index * row_step, row_step), row_step)
        rows = rows_ref[at, :]
        gate = lax.dot_general(rows, gate_ref[...], over_width, preferred_element_type=jnp.float32)
        upward = lax.dot_general(rows, up_ref[...], over_width, preferred_element_type=jnp.float32)
        hidden = (gate * jax.nn.sigmoid(1.702 * gate) * (upward + 1.0)).astype(jnp.bfloat16)
        part = jnp.dot(hidden, down_ref[...], preferred_element_type=jnp.float32)

        @pl.when(step == 0)
        def _():
            total_ref[at, :] = part

        @pl.when((step > 0) & (step < last))
        def _():
            total_ref[at, :] += part

        @pl.when(step == last)
        def _():
            out_ref[at, :] = (total_ref[at, :] + part).astype(jnp.bfloat16)

        return carry

    lax.fori_loop(0, rows_ref.shape[0] // row_step, row_block, 0)


def expert_mlp(rows, gate_rows, up_rows, down_rows, tile, row_step):
    count, width = rows.shape
    units = gate_rows.shape[0]
    weight = pl.BlockSpec((tile, width), lambda i: (i, 0))
    whole = pl.BlockSpec((count, width), lambda i: (0, 0))
    return pl.pallas_call(
        functools.partial(expert_body, row_step),
        out_shape=jax.ShapeDtypeStruct((count, width), jnp.bfloat16),
        grid=(units // tile,),
        in_specs=[whole, weight, weight, weight],
        out_specs=whole,
        scratch_shapes=[pltpu.VMEM((count, width), jnp.float32)],
        compiler_params=pltpu.CompilerParams(vmem_limit_bytes=52 * 2**20),
        cost_estimate=pl.CostEstimate(
            flops=6 * count * width * units,
            bytes_accessed=6 * width * units + 4 * count * width,
            transcendentals=count * units,
        ),
    )(rows, gate_rows, up_rows, down_rows)


def shards(
    x_input,
    q_input,
    k_input,
    v_input,
    out_weight,
    norm_gain,
    expert_ids,
    route_weights,
    gate_weights,
    up_weights,
    down_weights,
):
    tok_rows = x_input.shape[1]
    width = x_input.shape[2]
    seq_count = lax.axis_size("seq")
    grp_count = lax.axis_size("grp")
    expert_count = seq_count * grp_count
    top_count = expert_ids.shape[2]
    slot_count = 2 * tok_rows * top_count // expert_count
    key_width = k_input.shape[2]
    heads_kv = key_width // HEAD
    group = q_input.shape[2] // key_width
    rim_rows = jnp.stack([k_input[0, tok_rows - WINDOW :], v_input[0, tok_rows - WINDOW :]])
    earlier = shifted(rim_rows, "seq", 1)
    key_rows = jnp.concatenate([earlier[0], k_input[0]], 0).reshape(
        WINDOW + tok_rows, heads_kv, HEAD
    )
    value_rows = jnp.concatenate([earlier[1], v_input[0]], 0).reshape(
        WINDOW + tok_rows, heads_kv, HEAD
    )
    query_rows = q_input[0].reshape(tok_rows, heads_kv, group, HEAD)
    scores = jnp.einsum(
        "tkgd,skd->kgts", query_rows, key_rows, preferred_element_type=jnp.float32
    ) * (1.0 / math.sqrt(HEAD))
    first = lax.axis_index("seq") * tok_rows
    query_pos = first + jnp.arange(tok_rows, dtype=jnp.int32)
    key_pos = first - WINDOW + jnp.arange(WINDOW + tok_rows, dtype=jnp.int32)
    attention = softmax_mix(scores, query_pos, key_pos, value_rows).reshape(
        tok_rows, heads_kv * group * HEAD
    )
    share = width // grp_count
    own_share = lax.dynamic_slice_in_dim(
        out_weight, lax.axis_index("grp") * share, share, 1
    )
    share_weight = lax.all_gather(own_share, "seq", axis=0, tiled=True)
    attention, share_weight = lax.optimization_barrier((attention, share_weight))
    line_attention = lax.all_gather(attention, "grp", axis=0, tiled=True)
    line_part = jnp.dot(
        line_attention, share_weight, preferred_element_type=jnp.float32
    ).astype(jnp.bfloat16)
    parts = lax.all_to_all(
        line_part.reshape(grp_count, tok_rows, share), "grp", split_axis=0, concat_axis=0, tiled=True
    )
    projected = jnp.swapaxes(parts, 0, 1).reshape(tok_rows, width)
    stream = x_input[0].astype(jnp.float32) + projected.astype(jnp.float32)
    mean_square = jnp.mean(stream * stream, axis=-1, keepdims=True)
    normed = (stream * lax.rsqrt(mean_square + 1e-05) * norm_gain).astype(jnp.bfloat16)

    named = expert_ids[0][:, :, None] == jnp.arange(expert_count, dtype=jnp.int32)[None, None, :]
    names = jnp.any(named, axis=1)
    expert_weight = jnp.sum(jnp.where(named, route_weights[0][:, :, None], 0.0), axis=1)
    tokens = jnp.arange(tok_rows, dtype=jnp.int32)
    before = (tokens[None, :] < tokens[:, None]).astype(jnp.bfloat16)
    rank = jnp.dot(
        before, names.astype(jnp.bfloat16), preferred_element_type=jnp.float32
    ).astype(jnp.int32)
    slots = jnp.arange(slot_count, dtype=jnp.int32)
    chosen = names[:, :, None] & (rank[:, :, None] == slots[None, None, :])
    mix = jnp.where(chosen, expert_weight[:, :, None], 0.0)
    mix_high = lax.reduce_precision(mix, 8, 7)
    mix_low = (mix - mix_high).astype(jnp.bfloat16)
    mix_high = mix_high.astype(jnp.bfloat16)

    gate_rows = jnp.swapaxes(gate_weights[0], 0, 1)
    up_rows = jnp.swapaxes(up_weights[0], 0, 1)
    tile = gate_rows.shape[0] // 3
    chunks = 2
    part_slots = slot_count // chunks
    part_rows = expert_count * part_slots
    mixture = jnp.zeros((), jnp.float32)
    for chunk in range(chunks):
        cut = slice(chunk * part_slots, (chunk + 1) * part_slots)
        select = chosen[:, :, cut].astype(jnp.bfloat16).reshape(tok_rows, part_rows)
        outgoing = lax.dot_general(
            select, normed, (((0,), (0,)), ((), ())), preferred_element_type=jnp.float32
        ).astype(jnp.bfloat16)
        received = lax.all_to_all(
            outgoing.reshape(expert_count, part_slots, width),
            ("seq", "grp"), split_axis=0, concat_axis=0, tiled=True,
        )
        served = expert_mlp(
            received.reshape(part_rows, width), gate_rows, up_rows, down_weights[0], tile,
            math.gcd(part_rows, 256),
        )
        returned = lax.all_to_all(
            served.reshape(expert_count, part_slots, width),
            ("seq", "grp"), split_axis=0, concat_axis=0, tiled=True,
        ).reshape(part_rows, width)
        for factors in (mix_high, mix_low):
            mixture = mixture + jnp.dot(
                factors[:, :, cut].reshape(tok_rows, part_rows), returned,
                preferred_element_type=jnp.float32,
            )
    return (stream + mixture).astype(jnp.bfloat16)[None]


def solution(mesh):
    placed = (
        P("grp", "seq", None),
        P("grp", "seq", None),
        P("grp", "seq", None),
        P("grp", "seq", None),
        P("seq", None),
        P(),
        P("grp", "seq", None),
        P("grp", "seq", None),
        P(("seq", "grp"), None, None),
        P(("seq", "grp"), None, None),
        P(("seq", "grp"), None, None),
    )
    return jax.shard_map(
        shards, mesh=mesh, in_specs=placed, out_specs=P("grp", "seq", None), check_vma=False
    )
```

```python
import functools
import math

import jax
import jax.numpy as jnp
from jax import lax
from jax.experimental import pallas as pl
from jax.experimental.pallas import tpu as pltpu
from jax.sharding import PartitionSpec as P

HEAD = 64
WINDOW = 128
PLANES = 4


def shifted(block, axis, distance):
    devices = range(lax.axis_size(axis))
    route = [(i - distance, i) for i in devices if i - distance in devices]
    return lax.ppermute(block, axis, route)


def softmax_mix(scores, query_pos, key_pos, value_block):
    allowed = (
        (key_pos[None, :] <= query_pos[:, None])
        & (key_pos[None, :] > query_pos[:, None] - WINDOW)
        & (key_pos[None, :] >= 0)
    )
    masked = jnp.where(allowed, scores, -jnp.inf)
    highest = jnp.max(masked, axis=-1, keepdims=True)
    powers = jnp.exp(masked - highest)
    weights = (powers / jnp.sum(powers, axis=-1, keepdims=True)).astype(jnp.bfloat16)
    return jnp.einsum(
        "kgts,skd->tkgd", weights, value_block, preferred_element_type=jnp.float32
    ).astype(jnp.bfloat16)


def expert_body(row_step, rows_ref, gate_ref, up_ref, down_ref, out_ref, total_ref):
    step = pl.program_id(0)
    last = pl.num_programs(0) - 1
    over_width = (((1,), (1,)), ((), ()))

    def row_block(index, carry):
        at = pl.ds(pl.multiple_of(index * row_step, row_step), row_step)
        rows = rows_ref[at, :]
        gate = lax.dot_general(rows, gate_ref[...], over_width, preferred_element_type=jnp.float32)
        upward = lax.dot_general(rows, up_ref[...], over_width, preferred_element_type=jnp.float32)
        hidden = (gate * jax.nn.sigmoid(1.702 * gate) * (upward + 1.0)).astype(jnp.bfloat16)
        part = jnp.dot(hidden, down_ref[...], preferred_element_type=jnp.float32)

        @pl.when(step == 0)
        def _():
            total_ref[at, :] = part

        @pl.when((step > 0) & (step < last))
        def _():
            total_ref[at, :] += part

        @pl.when(step == last)
        def _():
            out_ref[at, :] = (total_ref[at, :] + part).astype(jnp.bfloat16)

        return carry

    lax.fori_loop(0, rows_ref.shape[0] // row_step, row_block, 0)


def expert_mlp(rows, gate_rows, up_rows, down_rows, tile, row_step):
    count, width = rows.shape
    units = gate_rows.shape[0]
    weight = pl.BlockSpec((tile, width), lambda i: (i, 0))
    whole = pl.BlockSpec((count, width), lambda i: (0, 0))
    return pl.pallas_call(
        functools.partial(expert_body, row_step),
        out_shape=jax.ShapeDtypeStruct((count, width), jnp.bfloat16),
        grid=(units // tile,),
        in_specs=[whole, weight, weight, weight],
        out_specs=whole,
        scratch_shapes=[pltpu.VMEM((count, width), jnp.float32)],
        compiler_params=pltpu.CompilerParams(vmem_limit_bytes=52 * 2**20),
        cost_estimate=pl.CostEstimate(
            flops=6 * count * width * units,
            bytes_accessed=6 * width * units + 4 * count * width,
            transcendentals=count * units,
        ),
    )(rows, gate_rows, up_rows, down_rows)


def shards(
    x_input,
    q_input,
    k_input,
    v_input,
    out_weight,
    norm_gain,
    expert_ids,
    route_weights,
    gate_weights,
    up_weights,
    down_weights,
):
    tok_rows = x_input.shape[1]
    width = x_input.shape[2]
    seq_count = lax.axis_size("seq")
    grp_count = lax.axis_size("grp")
    expert_count = seq_count * grp_count
    top_count = expert_ids.shape[2]
    slot_count = 2 * tok_rows * top_count // expert_count
    key_width = k_input.shape[2]
    heads_kv = key_width // HEAD
    group = q_input.shape[2] // key_width
    rim_rows = jnp.stack([k_input[0, tok_rows - WINDOW :], v_input[0, tok_rows - WINDOW :]])
    earlier = shifted(rim_rows, "seq", 1)
    key_rows = jnp.concatenate([earlier[0], k_input[0]], 0).reshape(
        WINDOW + tok_rows, heads_kv, HEAD
    )
    value_rows = jnp.concatenate([earlier[1], v_input[0]], 0).reshape(
        WINDOW + tok_rows, heads_kv, HEAD
    )
    query_rows = q_input[0].reshape(tok_rows, heads_kv, group, HEAD)
    scores = jnp.einsum(
        "tkgd,skd->kgts", query_rows, key_rows, preferred_element_type=jnp.float32
    ) * (1.0 / math.sqrt(HEAD))
    first = lax.axis_index("seq") * tok_rows
    query_pos = first + jnp.arange(tok_rows, dtype=jnp.int32)
    key_pos = first - WINDOW + jnp.arange(WINDOW + tok_rows, dtype=jnp.int32)
    attention = softmax_mix(scores, query_pos, key_pos, value_rows).reshape(
        tok_rows, heads_kv * group * HEAD
    )
    share = width // grp_count
    own_share = lax.dynamic_slice_in_dim(
        out_weight, lax.axis_index("grp") * share, share, 1
    )
    share_weight = lax.all_gather(own_share, "seq", axis=0, tiled=True)
    line_attention = lax.all_to_all(
        jnp.broadcast_to(attention[None], (grp_count, *attention.shape)),
        "grp", split_axis=0, concat_axis=0, tiled=True,
    ).reshape(grp_count * tok_rows, attention.shape[1])
    line_part = jnp.dot(
        line_attention, share_weight, preferred_element_type=jnp.float32
    ).astype(jnp.bfloat16)
    parts = lax.all_to_all(
        line_part.reshape(grp_count, tok_rows, share), "grp", split_axis=0, concat_axis=0, tiled=True
    )
    projected = jnp.swapaxes(parts, 0, 1).reshape(tok_rows, width)
    stream = x_input[0].astype(jnp.float32) + projected.astype(jnp.float32)
    mean_square = jnp.mean(stream * stream, axis=-1, keepdims=True)
    normed = (stream * lax.rsqrt(mean_square + 1e-05) * norm_gain).astype(jnp.bfloat16)

    gate_rows = jnp.swapaxes(gate_weights[0], 0, 1)
    up_rows = jnp.swapaxes(up_weights[0], 0, 1)
    tile = gate_rows.shape[0] // 3
    lanes = seq_count // PLANES
    places = [(plane, lane) for plane in range(PLANES) for lane in range(lanes)]
    at = {place: place[0] * lanes + place[1] for place in places}
    up_plane = [(at[p, q], at[(p + 1) % PLANES, q]) for p, q in places]

    def lane_route(shift):
        return [(at[p, q], at[p, (q + shift) % lanes]) for p, q in places]

    seq_index = lax.axis_index("seq")
    plane, lane = seq_index // lanes, lax.rem(seq_index, lanes)
    choices = lax.all_gather(
        jnp.concatenate([expert_ids[0].astype(jnp.float32), route_weights[0]], 1), "seq"
    )
    local_experts = seq_index * grp_count + jnp.arange(grp_count, dtype=jnp.int32)
    tokens = jnp.arange(tok_rows, dtype=jnp.int32)
    before = (tokens[None, :] < tokens[:, None]).astype(jnp.bfloat16)
    slots = jnp.arange(slot_count, dtype=jnp.int32)
    block_rows = grp_count * slot_count

    def block_routes(steps, shift):
        source = lax.rem(plane + PLANES - steps, PLANES) * lanes + lax.rem(lane + lanes - shift, lanes)
        block = lax.dynamic_index_in_dim(choices, source, 0, keepdims=False)
        ids = block[:, :top_count].astype(jnp.int32)
        named = ids[:, :, None] == local_experts[None, None, :]
        names = jnp.any(named, axis=1)
        weight = jnp.sum(jnp.where(named, block[:, top_count:, None], 0.0), axis=1)
        rank = jnp.dot(
            before, names.astype(jnp.bfloat16), preferred_element_type=jnp.float32
        ).astype(jnp.int32)
        chosen = names[:, :, None] & (rank[:, :, None] == slots[None, None, :])
        mix = jnp.where(chosen, weight[:, :, None], 0.0).reshape(tok_rows, block_rows)
        high = lax.reduce_precision(mix, 8, 7)
        low = (mix - high).astype(jnp.bfloat16)
        select = chosen.reshape(tok_rows, block_rows).astype(jnp.bfloat16)
        return select, jnp.concatenate([high.astype(jnp.bfloat16), low], 1)

    routes = [[block_routes(k, j) for j in range(lanes)] for k in range(PLANES)]
    held = normed
    totals = []
    for k in range(PLANES):
        if k > 0:
            held = lax.ppermute(held, "seq", up_plane)
        outgoing = []
        for j in range(lanes):
            block = held if j == 0 else lax.ppermute(held, "seq", lane_route(j))
            outgoing.append(
                lax.dot_general(
                    routes[k][j][0], block, (((0,), (0,)), ((), ())), preferred_element_type=jnp.float32
                ).astype(jnp.bfloat16).reshape(grp_count, slot_count, width)
            )
        received = lax.all_to_all(
            jnp.concatenate(outgoing, 1), "grp", split_axis=0, concat_axis=0, tiled=True
        )
        rows = grp_count * lanes * slot_count
        served = expert_mlp(
            received.reshape(rows, width), gate_rows, up_rows, down_weights[0], tile, math.gcd(rows, 256)
        )
        returned = lax.all_to_all(
            served.reshape(grp_count, lanes * slot_count, width),
            "grp", split_axis=0, concat_axis=0, tiled=True,
        ).reshape(grp_count, lanes, slot_count, width)
        total = jnp.zeros((), jnp.float32)
        for j in range(lanes):
            back = returned[:, j].reshape(block_rows, width)
            part = jnp.dot(
                routes[k][j][1], jnp.concatenate([back, back], 0), preferred_element_type=jnp.float32
            )
            if j > 0:
                part = lax.ppermute(
                    part.astype(jnp.bfloat16), "seq", lane_route(lanes - j)
                ).astype(jnp.float32)
            total = total + part
        totals.append(total)
    carried = totals[1]
    for k in range(2, PLANES + 1):
        carried = totals[k % PLANES] + lax.ppermute(
            carried.astype(jnp.bfloat16), "seq", up_plane
        ).astype(jnp.float32)
    return (stream + carried).astype(jnp.bfloat16)[None]


def solution(mesh):
    placed = (
        P("grp", "seq", None),
        P("grp", "seq", None),
        P("grp", "seq", None),
        P("grp", "seq", None),
        P("seq", None),
        P(),
        P("grp", "seq", None),
        P("grp", "seq", None),
        P(("seq", "grp"), None, None),
        P(("seq", "grp"), None, None),
        P(("seq", "grp"), None, None),
    )
    return jax.shard_map(
        shards, mesh=mesh, in_specs=placed, out_specs=P("grp", "seq", None), check_vma=False
    )
```

```python
import functools
import math

import jax
import jax.numpy as jnp
from jax import lax
from jax.experimental import pallas as pl
from jax.experimental.pallas import tpu as pltpu
from jax.sharding import PartitionSpec as P

HEAD = 64
WINDOW = 128
PLANES = 4


def shifted(block, axis, distance):
    devices = range(lax.axis_size(axis))
    route = [(i - distance, i) for i in devices if i - distance in devices]
    return lax.ppermute(block, axis, route)


def softmax_mix(scores, query_pos, key_pos, value_block):
    allowed = (
        (key_pos[None, :] <= query_pos[:, None])
        & (key_pos[None, :] > query_pos[:, None] - WINDOW)
        & (key_pos[None, :] >= 0)
    )
    masked = jnp.where(allowed, scores, -jnp.inf)
    highest = jnp.max(masked, axis=-1, keepdims=True)
    powers = jnp.exp(masked - highest)
    weights = (powers / jnp.sum(powers, axis=-1, keepdims=True)).astype(jnp.bfloat16)
    return jnp.einsum(
        "kgts,skd->tkgd", weights, value_block, preferred_element_type=jnp.float32
    ).astype(jnp.bfloat16)


def expert_body(row_step, rows_ref, gate_ref, up_ref, down_ref, out_ref, total_ref):
    step = pl.program_id(0)
    last = pl.num_programs(0) - 1
    over_width = (((1,), (1,)), ((), ()))

    def row_block(index, carry):
        at = pl.ds(pl.multiple_of(index * row_step, row_step), row_step)
        rows = rows_ref[at, :]
        gate = lax.dot_general(rows, gate_ref[...], over_width, preferred_element_type=jnp.float32)
        upward = lax.dot_general(rows, up_ref[...], over_width, preferred_element_type=jnp.float32)
        hidden = (gate * jax.nn.sigmoid(1.702 * gate) * (upward + 1.0)).astype(jnp.bfloat16)
        part = jnp.dot(hidden, down_ref[...], preferred_element_type=jnp.float32)

        @pl.when(step == 0)
        def _():
            total_ref[at, :] = part

        @pl.when((step > 0) & (step < last))
        def _():
            total_ref[at, :] += part

        @pl.when(step == last)
        def _():
            out_ref[at, :] = (total_ref[at, :] + part).astype(jnp.bfloat16)

        return carry

    lax.fori_loop(0, rows_ref.shape[0] // row_step, row_block, 0)


def expert_mlp(rows, gate_rows, up_rows, down_rows, tile, row_step):
    count, width = rows.shape
    units = gate_rows.shape[0]
    weight = pl.BlockSpec((tile, width), lambda i: (i, 0))
    whole = pl.BlockSpec((count, width), lambda i: (0, 0))
    return pl.pallas_call(
        functools.partial(expert_body, row_step),
        out_shape=jax.ShapeDtypeStruct((count, width), jnp.bfloat16),
        grid=(units // tile,),
        in_specs=[whole, weight, weight, weight],
        out_specs=whole,
        scratch_shapes=[pltpu.VMEM((count, width), jnp.float32)],
        compiler_params=pltpu.CompilerParams(vmem_limit_bytes=52 * 2**20),
        cost_estimate=pl.CostEstimate(
            flops=6 * count * width * units,
            bytes_accessed=6 * width * units + 4 * count * width,
            transcendentals=count * units,
        ),
    )(rows, gate_rows, up_rows, down_rows)


def shards(
    x_input,
    q_input,
    k_input,
    v_input,
    out_weight,
    norm_gain,
    expert_ids,
    route_weights,
    gate_weights,
    up_weights,
    down_weights,
):
    tok_rows = x_input.shape[1]
    width = x_input.shape[2]
    seq_count = lax.axis_size("seq")
    grp_count = lax.axis_size("grp")
    expert_count = seq_count * grp_count
    top_count = expert_ids.shape[2]
    slot_count = 2 * tok_rows * top_count // expert_count
    key_width = k_input.shape[2]
    heads_kv = key_width // HEAD
    group = q_input.shape[2] // key_width
    rim_rows = jnp.stack([k_input[0, tok_rows - WINDOW :], v_input[0, tok_rows - WINDOW :]])
    earlier = shifted(rim_rows, "seq", 1)
    key_rows = jnp.concatenate([earlier[0], k_input[0]], 0).reshape(
        WINDOW + tok_rows, heads_kv, HEAD
    )
    value_rows = jnp.concatenate([earlier[1], v_input[0]], 0).reshape(
        WINDOW + tok_rows, heads_kv, HEAD
    )
    query_rows = q_input[0].reshape(tok_rows, heads_kv, group, HEAD)
    scores = jnp.einsum(
        "tkgd,skd->kgts", query_rows, key_rows, preferred_element_type=jnp.float32
    ) * (1.0 / math.sqrt(HEAD))
    first = lax.axis_index("seq") * tok_rows
    query_pos = first + jnp.arange(tok_rows, dtype=jnp.int32)
    key_pos = first - WINDOW + jnp.arange(WINDOW + tok_rows, dtype=jnp.int32)
    attention = softmax_mix(scores, query_pos, key_pos, value_rows).reshape(
        tok_rows, heads_kv * group * HEAD
    )
    share = width // grp_count
    own_share = lax.dynamic_slice_in_dim(
        out_weight, lax.axis_index("grp") * share, share, 1
    )
    share_weight = lax.all_gather(own_share, "seq", axis=0, tiled=True)
    line_attention = lax.all_to_all(
        jnp.broadcast_to(attention[None], (grp_count, *attention.shape)),
        "grp", split_axis=0, concat_axis=0, tiled=True,
    ).reshape(grp_count * tok_rows, attention.shape[1])
    line_part = jnp.dot(
        line_attention, share_weight, preferred_element_type=jnp.float32
    ).astype(jnp.bfloat16)
    parts = lax.all_to_all(
        line_part.reshape(grp_count, tok_rows, share), "grp", split_axis=0, concat_axis=0, tiled=True
    )
    projected = jnp.swapaxes(parts, 0, 1).reshape(tok_rows, width)
    stream = x_input[0].astype(jnp.float32) + projected.astype(jnp.float32)
    mean_square = jnp.mean(stream * stream, axis=-1, keepdims=True)
    normed = (stream * lax.rsqrt(mean_square + 1e-05) * norm_gain).astype(jnp.bfloat16)

    gate_rows = jnp.swapaxes(gate_weights[0], 0, 1)
    up_rows = jnp.swapaxes(up_weights[0], 0, 1)
    tile = gate_rows.shape[0] // 3
    lanes = seq_count // PLANES
    places = [(plane, lane) for plane in range(PLANES) for lane in range(lanes)]
    at = {place: place[0] * lanes + place[1] for place in places}
    up_plane = [(at[p, q], at[(p + 1) % PLANES, q]) for p, q in places]

    def lane_route(shift):
        return [(at[p, q], at[p, (q + shift) % lanes]) for p, q in places]

    seq_index = lax.axis_index("seq")
    plane, lane = seq_index // lanes, lax.rem(seq_index, lanes)
    own_choices = jnp.concatenate([expert_ids[0].astype(jnp.float32), route_weights[0]], 1)
    choices = lax.all_to_all(
        jnp.broadcast_to(own_choices[None], (seq_count, *own_choices.shape)),
        "seq", split_axis=0, concat_axis=0, tiled=True,
    )
    local_experts = seq_index * grp_count + jnp.arange(grp_count, dtype=jnp.int32)
    tokens = jnp.arange(tok_rows, dtype=jnp.int32)
    before = (tokens[None, :] < tokens[:, None]).astype(jnp.bfloat16)
    slots = jnp.arange(slot_count, dtype=jnp.int32)
    block_rows = grp_count * slot_count

    def block_routes(steps, shift):
        source = lax.rem(plane + PLANES - steps, PLANES) * lanes + lax.rem(lane + lanes - shift, lanes)
        block = lax.dynamic_index_in_dim(choices, source, 0, keepdims=False)
        ids = block[:, :top_count].astype(jnp.int32)
        named = ids[:, :, None] == local_experts[None, None, :]
        names = jnp.any(named, axis=1)
        weight = jnp.sum(jnp.where(named, block[:, top_count:, None], 0.0), axis=1)
        rank = jnp.dot(
            before, names.astype(jnp.bfloat16), preferred_element_type=jnp.float32
        ).astype(jnp.int32)
        chosen = names[:, :, None] & (rank[:, :, None] == slots[None, None, :])
        mix = jnp.where(chosen, weight[:, :, None], 0.0).reshape(tok_rows, block_rows)
        high = lax.reduce_precision(mix, 8, 7)
        low = (mix - high).astype(jnp.bfloat16)
        select = chosen.reshape(tok_rows, block_rows).astype(jnp.bfloat16)
        return select, jnp.concatenate([high.astype(jnp.bfloat16), low], 1)

    routes = [[block_routes(k, j) for j in range(lanes)] for k in range(PLANES)]
    held = normed
    totals = []
    for k in range(PLANES):
        if k > 0:
            held = lax.ppermute(held, "seq", up_plane)
        outgoing = []
        for j in range(lanes):
            block = held if j == 0 else lax.ppermute(held, "seq", lane_route(j))
            outgoing.append(
                lax.dot_general(
                    routes[k][j][0], block, (((0,), (0,)), ((), ())), preferred_element_type=jnp.float32
                ).astype(jnp.bfloat16).reshape(grp_count, slot_count, width)
            )
        received = lax.all_to_all(
            jnp.concatenate(outgoing, 1), "grp", split_axis=0, concat_axis=0, tiled=True
        )
        rows = grp_count * lanes * slot_count
        served = expert_mlp(
            received.reshape(rows, width), gate_rows, up_rows, down_weights[0], tile, math.gcd(rows, 256)
        )
        returned = lax.all_to_all(
            served.reshape(grp_count, lanes * slot_count, width),
            "grp", split_axis=0, concat_axis=0, tiled=True,
        ).reshape(grp_count, lanes, slot_count, width)
        total = jnp.zeros((), jnp.float32)
        for j in range(lanes):
            back = returned[:, j].reshape(block_rows, width)
            part = jnp.dot(
                routes[k][j][1], jnp.concatenate([back, back], 0), preferred_element_type=jnp.float32
            )
            if j > 0:
                part = lax.ppermute(
                    part.astype(jnp.bfloat16), "seq", lane_route(lanes - j)
                ).astype(jnp.float32)
            total = total + part
        totals.append(total)
    carried = totals[1]
    for k in range(2, PLANES + 1):
        carried = totals[k % PLANES] + lax.ppermute(
            carried.astype(jnp.bfloat16), "seq", up_plane
        ).astype(jnp.float32)
    return (stream + carried).astype(jnp.bfloat16)[None]


def solution(mesh):
    placed = (
        P("grp", "seq", None),
        P("grp", "seq", None),
        P("grp", "seq", None),
        P("grp", "seq", None),
        P("seq", None),
        P(),
        P("grp", "seq", None),
        P("grp", "seq", None),
        P(("seq", "grp"), None, None),
        P(("seq", "grp"), None, None),
        P(("seq", "grp"), None, None),
    )
    return jax.shard_map(
        shards, mesh=mesh, in_specs=placed, out_specs=P("grp", "seq", None), check_vma=False
    )
```
